512 devices in a mesh: ctx: 32 (over x, z_lo), dp: 16 (over y, z_hi, core).
Axes of the slice: x: 4, y: 4, z: 16 (z_hi: 2, z_lo: 8; z = z_hi * 8 + z_lo), core: 2. Of those that a mesh axis runs over, the one named last changes fastest.
Arguments:
- queries: bfloat16 [16, 4096, 2560], P('dp', 'ctx'), may hold values from -8 to 8
- keys: bfloat16 [16, 4096, 512], P('dp', 'ctx'), may hold values from -6 to 6
- values: bfloat16 [16, 4096, 512], P('dp', 'ctx'), may hold values from -6 to 6
- output_gradient: bfloat16 [16, 4096, 2560], P('dp', 'ctx'), may hold values from -6 to 6
- inputs: bfloat16 [16, 4096, 5120], P('dp', 'ctx'), may hold values from -6 to 6
- span_ids: int32 [64], P('ctx'), may hold values from 0 to 63, as said below
- segments: int32 [16, 4096], P('dp'), may hold values from 0 to 7, never falling along the last dimension, each value on 1 to 1024 neighbouring positions
Outputs:
- grad_queries: bfloat16 [16, 4096, 2560], P('dp', 'ctx')
- grad_wk: float32 [5120, 512], P('ctx')
- grad_wv: float32 [5120, 512], P('ctx')
The draws below stay inside these ranges and needn't reach their ends.
Inputs may be any that keep to these rules, and one draw needn't show every extreme that they name: span_ids[2 r + 1] = 63 - span_ids[2 r] for every r, and each number appears once.
All inputs are finite; a program needn't handle non-finite values.
Results may differ from the reference program's by a relative error of at most 0.025.
Values may be sent and summed in bfloat16 or wider, within the bound.
No kernel may reach another device: no remote copies, remote signals or barrier semaphores. Data moves between devices by JAX's collectives and lax.ppermute only.
A program may use at most 64 MiB of HBM per device.

```python
import math
import jax
import jax.numpy as jnp
import numpy as np
from jax import lax

MODEL_WIDTH = 5120
QUERY_HEADS = 20
KEY_VALUE_HEADS = 4
HEAD_SIZE = 128
TOK_DEV = 128
WINDOW = 4
SEQUENCE_LENGTH = 4096
SEQUENCE_COUNT = 16
N_CTX = 32


def draw_keys(key, part):
    key = jax.random.fold_in(key, 3)
    complete_shape = (SEQUENCE_COUNT, SEQUENCE_LENGTH, KEY_VALUE_HEADS * HEAD_SIZE)
    return jnp.clip(jax.random.normal(key, complete_shape, jnp.float32), -6.0, 6.0).astype(jnp.bfloat16)


def draw_queries(key, part):
    key = jax.random.fold_in(key, 5)
    complete_shape = (SEQUENCE_COUNT, SEQUENCE_LENGTH, QUERY_HEADS * HEAD_SIZE)
    return jnp.clip(jax.random.normal(key, complete_shape, jnp.float32), -6.0, 6.0).astype(jnp.bfloat16)


def draw_span_ids(key, part):
    key = jax.random.fold_in(key, 9)
    cycle_length = SEQUENCE_LENGTH // TOK_DEV
    order = jax.random.permutation(key, cycle_length).astype(jnp.int32)
    return jnp.stack([order, 2 * cycle_length - 1 - order], axis=1).reshape(-1)


def level_of(rng, extent, pieces, least, largest):
    level, own = 1.0, jax.random.fold_in(rng, 6)
    for dim, blocks in pieces:
        heights = jnp.exp(jax.random.uniform(jax.random.fold_in(own, dim), (blocks,), jnp.float32, least / len(pieces), largest / len(pieces)))
        level = level * jnp.repeat(heights, extent[dim] // blocks).reshape([-1 if axis == dim else 1 for axis in range(len(extent))])
    return level


def profile(count, total, reach, slope):
    portions = [(1 << 20) // math.isqrt(grade ** slope) + 1 for grade in range(2, count + 1)]
    rest, given = total - reach - (count - 1), [1] * (count - 1)
    while rest > 0:
        candidates = [i for i in range(count - 1) if given[i] < reach]
        pool, budget = sum([portions[i] for i in candidates]), rest
        for i in candidates:
            more = min(reach - given[i], max(1, budget * portions[i] // pool), rest)
            given[i] = given[i] + more
            rest = rest - more
    return np.array([reach] + given)


def ragged(own_key, number_of, total, limit, skew):
    if number_of == 2:
        one = jax.random.randint(own_key, (), max(1, total - limit), min(limit, total - 1) + 1)
        return jnp.stack([one, total - one])
    sizes = jnp.asarray(profile(number_of, total, limit, skew), jnp.int32)
    twos = (number_of - 1) // 2
    donor, taker = sizes[1:1 + 2 * twos:2], sizes[2:2 + 2 * twos:2]
    slack = jnp.minimum(donor - 1, limit - taker)
    passed = jax.random.randint(jax.random.fold_in(own_key, 1), (twos,), 0, 1 << 20) % (slack + 1)
    sizes = sizes.at[1:1 + 2 * twos:2].set(donor - passed).at[2:2 + 2 * twos:2].set(taker + passed)
    return sizes[jax.random.permutation(jax.random.fold_in(own_key, 2), number_of)]


def centred(key, extent, deviation, most, pieces=(), kind=jnp.bfloat16):
    factor_of = level_of(key, extent, pieces, -0.22, 0.18) if pieces else 1.0
    result = jax.random.normal(key, extent, jnp.float32) * deviation * factor_of
    return jnp.minimum(jnp.maximum(result, -most), most).astype(kind)


def setup_inputs(seed: int = 0) -> dict:
    arg_keys = jax.random.split(jax.random.key(seed), 8)
    return {
        "queries": draw_queries(jax.random.fold_in(arg_keys[7], 71), 0),
        "keys": draw_keys(jax.random.fold_in(arg_keys[7], 71), 0),
        "values": centred(arg_keys[2], (SEQUENCE_COUNT, SEQUENCE_LENGTH, KEY_VALUE_HEADS * HEAD_SIZE), 1.0, 6.0, ((0, 16), (1, 32))),
        "output_gradient": centred(arg_keys[3], (SEQUENCE_COUNT, SEQUENCE_LENGTH, QUERY_HEADS * HEAD_SIZE), 1.0, 6.0, ((0, 16), (1, 32))),
        "inputs": centred(arg_keys[4], (SEQUENCE_COUNT, SEQUENCE_LENGTH, MODEL_WIDTH), 1.0, 6.0, ((0, 16), (1, 32))),
        "span_ids": draw_span_ids(jax.random.fold_in(arg_keys[7], 71), 0),
        "segments": jax.vmap(lambda own: jnp.searchsorted(jnp.cumsum(ragged(own, 8, SEQUENCE_LENGTH, SEQUENCE_LENGTH // 4, 1)), jnp.arange(SEQUENCE_LENGTH), side="right"))(jax.random.split(arg_keys[6], SEQUENCE_COUNT)).reshape((SEQUENCE_COUNT, SEQUENCE_LENGTH)).astype(jnp.int32),
    }


def window_span(array):
    return jnp.stack([jnp.roll(array, cycle_offset, axis=0) for cycle_offset in range(WINDOW)], axis=1)


def reference(queries, keys, values, output_gradient, inputs, span_ids, segments):
    cycle_length = N_CTX
    token_rows = TOK_DEV
    half_rows = token_rows // 2
    sharing_queries = QUERY_HEADS // KEY_VALUE_HEADS
    score_scale = HEAD_SIZE ** -0.5
    row_index = jnp.arange(token_rows, dtype=jnp.int32)
    pairs = span_ids.reshape(cycle_length, 2).astype(jnp.int32)
    position = jnp.where(row_index[None, :] < half_rows, pairs[:, 0:1], pairs[:, 1:2]) * half_rows + row_index[None, :] % half_rows
    key_position = window_span(position)

    def per_sequence(carry, item):
        query_matrix, key_row_block, value_row_block, gradient_rows, input_rows, doc_ids = item
        query_wide = query_matrix.reshape(cycle_length, token_rows, KEY_VALUE_HEADS, sharing_queries, HEAD_SIZE).astype(jnp.float32)
        gradient_wide = gradient_rows.reshape(cycle_length, token_rows, KEY_VALUE_HEADS, sharing_queries, HEAD_SIZE).astype(jnp.float32)
        key_wide = window_span(key_row_block.reshape(cycle_length, token_rows, KEY_VALUE_HEADS, HEAD_SIZE)).astype(jnp.float32)
        value_wide = window_span(value_row_block.reshape(cycle_length, token_rows, KEY_VALUE_HEADS, HEAD_SIZE)).astype(jnp.float32)
        doc_query = doc_ids[position]
        doc_key = doc_ids[key_position]
        allowed = (key_position[:, None, :, :] <= position[:, :, None, None]) & (doc_key[:, None, :, :] == doc_query[:, :, None, None])
        allowed = allowed[:, None, None]
        scores = jnp.einsum('rtgcd,rwsgd->rgctws', query_wide, key_wide) * score_scale
        scores = jnp.where(allowed, scores, -1e30)
        peak = jnp.max(scores, axis=(4, 5), keepdims=True)
        expd = jnp.where(allowed, jnp.exp(scores - peak), 0.0)
        probs = expd / jnp.sum(expd, axis=(4, 5), keepdims=True)
        probs_b = lax.optimization_barrier(probs.astype(jnp.bfloat16)).astype(jnp.float32)
        out = jnp.einsum('rgctws,rwsgd->rtgcd', probs_b, value_wide).astype(jnp.bfloat16)
        out_f = lax.optimization_barrier(out).astype(jnp.float32)
        delta = jnp.einsum('rtgc->rgct', jnp.sum(gradient_wide * out_f, axis=-1))
        dprobs = jnp.einsum('rtgcd,rwsgd->rgctws', gradient_wide, value_wide)
        dscores = probs * (dprobs - delta[..., None, None])
        dscores_b = lax.optimization_barrier(dscores.astype(jnp.bfloat16)).astype(jnp.float32)
        grad_query = (jnp.einsum('rgctws,rwsgd->rtgcd', dscores_b, key_wide) * score_scale).astype(jnp.bfloat16)
        dkeys_w = jnp.einsum('rgctws,rtgcd->rwsgd', dscores_b, query_wide) * score_scale
        dvalues_w = jnp.einsum('rgctws,rtgcd->rwsgd', probs_b, gradient_wide)
        key_gradients = sum(jnp.roll(dkeys_w[:, cycle_offset], -cycle_offset, axis=0) for cycle_offset in range(WINDOW))
        value_gradients = sum(jnp.roll(dvalues_w[:, cycle_offset], -cycle_offset, axis=0) for cycle_offset in range(WINDOW))
        key_gradients = key_gradients.reshape(cycle_length * token_rows, KEY_VALUE_HEADS * HEAD_SIZE).astype(jnp.bfloat16)
        value_gradients = value_gradients.reshape(cycle_length * token_rows, KEY_VALUE_HEADS * HEAD_SIZE).astype(jnp.bfloat16)
        new_k = carry[0] + jnp.dot(input_rows.T, key_gradients, preferred_element_type=jnp.float32)
        new_v = carry[1] + jnp.dot(input_rows.T, value_gradients, preferred_element_type=jnp.float32)
        return (new_k, new_v), grad_query.reshape(cycle_length * token_rows, QUERY_HEADS * HEAD_SIZE)

    start_position = (jnp.zeros((MODEL_WIDTH, KEY_VALUE_HEADS * HEAD_SIZE), jnp.float32), jnp.zeros((MODEL_WIDTH, KEY_VALUE_HEADS * HEAD_SIZE), jnp.float32))
    (grad_wk, grad_wv), grad_queries = lax.scan(per_sequence, start_position, (queries, keys, values, output_gradient, inputs, segments))
    return grad_queries, grad_wk, grad_wv
```

```python
import functools
import math

import jax
import jax.numpy as jnp
from jax import lax
from jax.experimental import pallas as pl
from jax.experimental.pallas import tpu as pltpu
from jax.sharding import Mesh, PartitionSpec as P

QUERY_HEADS = 20
KEY_VALUE_HEADS = 4
SHARING = QUERY_HEADS // KEY_VALUE_HEADS
HEAD = 128
ROWS = 128
HALF = ROWS // 2
WINDOW = 4
DOCUMENTS = 8
SCALE = HEAD ** (-0.5)
CTX = ("x", "zl")
DP = ("y", "zh", "c")
BF16 = jnp.bfloat16
F32 = jnp.float32


def shifted(block, distance):
    n = lax.axis_size(CTX)
    return lax.ppermute(block, CTX, [((i - distance) % n, i) for i in range(n)])


def exchange(blocks, axes):
    return lax.all_to_all(blocks, axes, 0, 0, tiled=True)


def dot(a, b, ca, cb):
    return lax.dot_general(a, b, (((ca,), (cb,)), ((), ())), preferred_element_type=F32)


def attention_kernel(
    span_ref, seg_ref, q_ref, g_ref, k_ref, v_ref, t1_ref, t2_ref, t3_ref,
    dq_ref, own_ref, r1_ref, r2_ref, r3_ref, bias_ref,
):
    tiles = (t1_ref, t2_ref, t3_ref)

    @pl.when(pl.program_id(0) == 0)
    def _():
        lane = lax.broadcasted_iota(jnp.int32, (1, ROWS), 1)
        pos_q = jnp.where(lane < HALF, span_ref[0] * HALF + lane, span_ref[1] * HALF + lane - HALF)
        seg = seg_ref[...]
        start = jnp.zeros((1, ROWS), jnp.int32)
        for doc in range(1, DOCUMENTS):
            first = jnp.sum((seg < doc).astype(F32), axis=1, keepdims=True).astype(jnp.int32)
            start = jnp.maximum(start, jnp.where(first <= pos_q, first, 0))
        row = lax.broadcasted_iota(jnp.int32, (HALF, ROWS), 0)
        for step in range(WINDOW):
            for half in range(2):
                if step == 0:
                    span = span_ref[half]
                else:
                    at = 2 * ROWS + 8 * half
                    span = tiles[step - 1][at : at + 8, :].astype(F32)[0:1, :].astype(jnp.int32)
                pos_k = span * HALF + row
                allowed = (pos_k <= pos_q) & (pos_k >= start)
                at = step * ROWS + half * HALF
                bias_ref[at : at + HALF, :] = jnp.where(allowed, 0.0, -1e30)

    k = jnp.concatenate([k_ref[...]] + [t[0:ROWS, :] for t in tiles], axis=0)
    v = jnp.concatenate([v_ref[...]] + [t[ROWS : 2 * ROWS, :] for t in tiles], axis=0)
    heads = [slice(c * HEAD, (c + 1) * HEAD) for c in range(SHARING)]
    q = jnp.concatenate([q_ref[:, h] for h in heads], axis=0)
    g = jnp.concatenate([g_ref[:, h] for h in heads], axis=0)
    bias = bias_ref[...]
    s = dot(k, q, 1, 1) + jnp.concatenate([bias] * SHARING, axis=1)
    e = jnp.exp2((s - jnp.max(s, axis=0, keepdims=True)) * (SCALE * math.log2(math.e)))
    p = e * (1.0 / jnp.sum(e, axis=0, keepdims=True))
    dp = dot(v, g, 1, 1)
    delta = jnp.sum(p * dp, axis=0, keepdims=True)
    ds = (p * (dp - delta)).astype(BF16)
    dv = dot(p.astype(BF16), g, 1, 0)
    dk = dot(ds, q, 1, 0) * SCALE
    dq = (dot(ds, k, 0, 0) * SCALE).astype(BF16)
    for c, h in enumerate(heads):
        dq_ref[:, h] = dq[c * ROWS : (c + 1) * ROWS, :]
    own_ref[0] = dk[0:ROWS]
    own_ref[1] = dv[0:ROWS]
    for step, ref in enumerate((r1_ref, r2_ref, r3_ref), 1):
        rows = slice(step * ROWS, (step + 1) * ROWS)
        ref[0] = dk[rows].astype(BF16)
        ref[1] = dv[rows].astype(BF16)


def attention(span, segments, queries, gradient, keys, values, tiles):
    wide = pl.BlockSpec((None, ROWS, SHARING * HEAD), lambda i: (0, 0, i))
    narrow = pl.BlockSpec((None, ROWS, HEAD), lambda i: (0, 0, i))
    tile = pl.BlockSpec((tiles[0].shape[0], HEAD), lambda i: (0, i))
    term = pl.BlockSpec((2, None, ROWS, HEAD), lambda i: (0, i // 2, 0, i % 2))
    terms = (2, 2, ROWS, 2 * HEAD)
    work = QUERY_HEADS * ROWS * WINDOW * ROWS
    return pl.pallas_call(
        attention_kernel,
        grid=(KEY_VALUE_HEADS,),
        in_specs=[
            pl.BlockSpec(memory_space=pltpu.SMEM),
            pl.BlockSpec(segments.shape, lambda i: (0, 0)),
            wide, wide, narrow, narrow, tile, tile, tile,
        ],
        out_specs=[wide, term, term, term, term],
        out_shape=[
            jax.ShapeDtypeStruct(queries.shape, BF16),
            jax.ShapeDtypeStruct(terms, F32),
            jax.ShapeDtypeStruct(terms, BF16),
            jax.ShapeDtypeStruct(terms, BF16),
            jax.ShapeDtypeStruct(terms, BF16),
        ],
        scratch_shapes=[pltpu.VMEM((WINDOW * ROWS, ROWS), F32)],
        compiler_params=pltpu.CompilerParams(vmem_limit_bytes=48 * 1024 * 1024),
        cost_estimate=pl.CostEstimate(
            flops=10 * HEAD * work, bytes_accessed=5 * 1024 * 1024, transcendentals=work
        ),
        name="attention",
    )(span, segments, queries, gradient, keys, values, *tiles)


def on_device(queries, keys, values, output_gradient, inputs, span_ids, segments):
    nx, ny, nzl, nzh, nc = (lax.axis_size(a) for a in ("x", "y", "zl", "zh", "c"))
    rows, features = inputs.shape[1:]
    part = features // nx
    with jax.named_scope("inputs_exchange"):
        by_x = inputs[0].reshape(rows, nx, part).transpose(1, 0, 2)
        blocks = jnp.broadcast_to(by_x[:, None], (nx, ny, rows, part)).reshape(nx * ny, rows, part)
        features_x = exchange(blocks, ("x", "y")).reshape(nx * ny * rows, part)
    with jax.named_scope("keys_values_halo"):
        numbers = jnp.broadcast_to(
            jnp.repeat(span_ids, 8, total_repeat_length=16)[:, None], (16, keys.shape[2])
        )
        tile = jnp.concatenate([keys[0], values[0], numbers.astype(BF16)], axis=0)
        tiles = [shifted(tile, step) for step in range(1, WINDOW)]
    with jax.named_scope("attention"):
        grad_queries, own, *terms = attention(
            span_ids, segments, queries, output_gradient, keys, values, tiles
        )
    with jax.named_scope("gradient_return"):
        back = [shifted(term, -step) for step, term in enumerate(terms, 1)]
        total = (own + sum(b.astype(F32) for b in back)).astype(BF16)
    with jax.named_scope("gradient_exchange"):
        by_y = total.reshape(ny, rows, 2 * HEAD)
        blocks = jnp.broadcast_to(by_y[None], (nx, ny, rows, 2 * HEAD))
        columns = exchange(blocks.reshape(nx * ny, rows, 2 * HEAD), ("x", "y"))
        columns = columns.reshape(nx * ny * rows, 2 * HEAD)
    with jax.named_scope("projection"):
        partial = dot(features_x, columns, 0, 0)
    with jax.named_scope("core_sum"):
        halves = partial.astype(BF16).reshape(part, nc, HEAD).transpose(1, 0, 2)
        pair = jnp.sum(exchange(halves, ("c",)).astype(F32), axis=0)
    with jax.named_scope("z_sum"):
        piece = part // (nzl * nzh)
        pieces = exchange(pair.astype(BF16).reshape(nzl * nzh, piece, HEAD), ("zl", "zh"))
        summed = jnp.sum(pieces.astype(F32), axis=0).astype(BF16)
    with jax.named_scope("replicate"):
        every = exchange(jnp.broadcast_to(summed[None], (ny * nzh * nc, piece, HEAD)), DP)
        every = every.reshape(ny, nzh, nc, piece, HEAD).transpose(1, 3, 0, 2, 4)
        every = every.reshape(nzh * piece, 2, ny * nc * HEAD // 2).astype(F32)
    return grad_queries, every[:, 0], every[:, 1]


def solution(mesh):
    axes = Mesh(mesh.devices.reshape(4, 8, 4, 2, 2), CTX + DP)
    by_row = P(DP, CTX, None)
    return jax.shard_map(
        on_device,
        mesh=axes,
        in_specs=(by_row, by_row, by_row, by_row, by_row, P(CTX), P(DP, None)),
        out_specs=(by_row, P(CTX, None), P(CTX, None)),
        check_vma=False,
    )
```

```python
import functools
import math

import jax
import jax.numpy as jnp
from jax import lax
from jax.experimental import pallas as pl
from jax.experimental.pallas import tpu as pltpu
from jax.sharding import Mesh, PartitionSpec as P

QUERY_HEADS = 20
KEY_VALUE_HEADS = 4
SHARING = QUERY_HEADS // KEY_VALUE_HEADS
HEAD = 128
ROWS = 128
HALF = ROWS // 2
WINDOW = 4
DOCUMENTS = 8
SCALE = HEAD ** (-0.5)
CTX = ("x", "zl")
DP = ("y", "zh", "c")
BF16 = jnp.bfloat16
VMEM_LIMIT = 60 * 1024 * 1024
F32 = jnp.float32


def shifted(block, distance):
    n = lax.axis_size(CTX)
    return lax.ppermute(block, CTX, [((i - distance) % n, i) for i in range(n)])


def exchange(blocks, axes):
    return lax.all_to_all(blocks, axes, 0, 0, tiled=True)


def dot(a, b, ca, cb):
    return lax.dot_general(a, b, (((ca,), (cb,)), ((), ())), preferred_element_type=F32)


def attention_kernel(
    span_ref, seg_ref, q_ref, g_ref, k_ref, v_ref, t1_ref, t2_ref, t3_ref,
    dq_ref, own_ref, r1_ref, r2_ref, r3_ref, bias_ref,
):
    tiles = (t1_ref, t2_ref, t3_ref)

    @pl.when(pl.program_id(0) == 0)
    def _():
        lane = lax.broadcasted_iota(jnp.int32, (1, ROWS), 1)
        pos_q = jnp.where(lane < HALF, span_ref[0] * HALF + lane, span_ref[1] * HALF + lane - HALF)
        seg = seg_ref[...]
        start = jnp.zeros((1, ROWS), jnp.int32)
        for doc in range(1, DOCUMENTS):
            first = jnp.sum((seg < doc).astype(F32), axis=1, keepdims=True).astype(jnp.int32)
            start = jnp.maximum(start, jnp.where(first <= pos_q, first, 0))
        row = lax.broadcasted_iota(jnp.int32, (HALF, ROWS), 0)
        for step in range(WINDOW):
            for half in range(2):
                if step == 0:
                    span = span_ref[half]
                else:
                    at = 2 * ROWS + 8 * half
                    span = tiles[step - 1][at : at + 8, :].astype(F32)[0:1, :].astype(jnp.int32)
                pos_k = span * HALF + row
                allowed = (pos_k <= pos_q) & (pos_k >= start)
                at = step * ROWS + half * HALF
                bias_ref[at : at + HALF, :] = jnp.where(allowed, 0.0, -1e30)

    k = jnp.concatenate([k_ref[...]] + [t[0:ROWS, :] for t in tiles], axis=0)
    v = jnp.concatenate([v_ref[...]] + [t[ROWS : 2 * ROWS, :] for t in tiles], axis=0)
    heads = [slice(c * HEAD, (c + 1) * HEAD) for c in range(SHARING)]
    q = jnp.concatenate([q_ref[:, h] for h in heads], axis=0)
    g = jnp.concatenate([g_ref[:, h] for h in heads], axis=0)
    bias = bias_ref[...]
    s = dot(k, q, 1, 1) + jnp.concatenate([bias] * SHARING, axis=1)
    e = jnp.exp2((s - jnp.max(s, axis=0, keepdims=True)) * (SCALE * math.log2(math.e)))
    p = e * (1.0 / jnp.sum(e, axis=0, keepdims=True))
    dp = dot(v, g, 1, 1)
    delta = jnp.sum(p * dp, axis=0, keepdims=True)
    ds = (p * (dp - delta)).astype(BF16)
    dv = dot(p.astype(BF16), g, 1, 0)
    dk = dot(ds, q, 1, 0) * SCALE
    dq = (dot(ds, k, 0, 0) * SCALE).astype(BF16)
    for c, h in enumerate(heads):
        dq_ref[:, h] = dq[c * ROWS : (c + 1) * ROWS, :]
    own_ref[0] = dk[0:ROWS]
    own_ref[1] = dv[0:ROWS]
    for step, ref in enumerate((r1_ref, r2_ref, r3_ref), 1):
        rows = slice(step * ROWS, (step + 1) * ROWS)
        ref[0] = dk[rows].astype(BF16)
        ref[1] = dv[rows].astype(BF16)


def sum_kernel(own_ref, b1_ref, b2_ref, b3_ref, after_ref, out_ref):
    del after_ref
    total = own_ref[...]
    for ref in (b1_ref, b2_ref, b3_ref):
        total = total + ref[...].astype(F32)
    out_ref[...] = total.astype(BF16)


def sum_terms(own, back, after):
    whole = pl.BlockSpec(memory_space=pltpu.VMEM)
    return pl.pallas_call(
        sum_kernel,
        in_specs=[whole] * 4 + [pl.BlockSpec(memory_space=pl.ANY)],
        out_specs=whole,
        out_shape=jax.ShapeDtypeStruct(own.shape, BF16),
        cost_estimate=pl.CostEstimate(flops=own.size * 4, bytes_accessed=own.size * 18, transcendentals=0),
        name="sum_terms",
    )(own, *back, after)


def attention(span, segments, queries, gradient, keys, values, tiles):
    wide = pl.BlockSpec((None, ROWS, SHARING * HEAD), lambda i: (0, 0, i))
    narrow = pl.BlockSpec((None, ROWS, HEAD), lambda i: (0, 0, i))
    tile = pl.BlockSpec((tiles[0].shape[0], HEAD), lambda i: (0, i))
    term = pl.BlockSpec((2, None, ROWS, HEAD), lambda i: (0, i // 2, 0, i % 2))
    terms = (2, 2, ROWS, 2 * HEAD)
    work = QUERY_HEADS * ROWS * WINDOW * ROWS
    return pl.pallas_call(
        attention_kernel,
        grid=(KEY_VALUE_HEADS,),
        in_specs=[
            pl.BlockSpec(memory_space=pltpu.SMEM),
            pl.BlockSpec(segments.shape, lambda i: (0, 0)),
            wide, wide, narrow, narrow, tile, tile, tile,
        ],
        out_specs=[wide, term, term, term, term],
        out_shape=[
            jax.ShapeDtypeStruct(queries.shape, BF16),
            jax.ShapeDtypeStruct(terms, F32),
            jax.ShapeDtypeStruct(terms, BF16),
            jax.ShapeDtypeStruct(terms, BF16),
            jax.ShapeDtypeStruct(terms, BF16),
        ],
        scratch_shapes=[pltpu.VMEM((WINDOW * ROWS, ROWS), F32)],
        compiler_params=pltpu.CompilerParams(vmem_limit_bytes=VMEM_LIMIT),
        cost_estimate=pl.CostEstimate(
            flops=10 * HEAD * work, bytes_accessed=5 * 1024 * 1024, transcendentals=work
        ),
        name="attention",
    )(span, segments, queries, gradient, keys, values, *tiles)


def on_device(queries, keys, values, output_gradient, inputs, span_ids, segments):
    nx, ny, nzl, nzh, nc = (lax.axis_size(a) for a in ("x", "y", "zl", "zh", "c"))
    rows, features = inputs.shape[1:]
    part = features // nx
    with jax.named_scope("keys_values_halo"):
        numbers = jnp.broadcast_to(span_ids.astype(BF16)[:, None, None], (2, 8, keys.shape[2]))
        tile = jnp.concatenate([keys[0], values[0], numbers.reshape(16, keys.shape[2])], axis=0)
        tiles = [shifted(tile, step) for step in range(1, WINDOW)]
    with jax.named_scope("inputs_exchange"):
        by_x = inputs[0].reshape(rows, nx, part).transpose(1, 0, 2)
        blocks = jnp.broadcast_to(by_x[:, None], (nx, ny, rows, part)).reshape(nx * ny, rows, part)
        features_x = exchange(blocks, ("x", "y")).reshape(nx * ny * rows, part)
    with jax.named_scope("attention"):
        grad_queries, own, *terms = attention(
            span_ids, segments, queries, output_gradient, keys, values, tiles
        )
    with jax.named_scope("gradient_return"):
        back = [shifted(term, -step) for step, term in enumerate(terms, 1)]
        blocks = sum_terms(own, back, features_x)
    with jax.named_scope("gradient_exchange"):
        blocks = jnp.broadcast_to(blocks.reshape(ny, rows, 2 * HEAD)[None], (nx, ny, rows, 2 * HEAD))
        columns = exchange(blocks.reshape(nx * ny, rows, 2 * HEAD), ("x", "y"))
        columns = columns.reshape(nx * ny * rows, 2 * HEAD)
    with jax.named_scope("projection"):
        partial = dot(features_x, columns, 0, 0)
    with jax.named_scope("core_sum"):
        halves = partial.astype(BF16).reshape(part, nc, HEAD).transpose(1, 0, 2)
        pair = jnp.sum(exchange(halves, ("c",)).astype(F32), axis=0)
    with jax.named_scope("z_sum"):
        piece = part // nzl
        pieces = exchange(pair.astype(BF16).reshape(nzl, piece, HEAD), ("zl",))
        summed = jnp.sum(pieces.astype(F32), axis=0).astype(BF16)
        other = lax.ppermute(summed, ("zh",), [(i, 1 - i) for i in range(nzh)])
        summed = (summed.astype(F32) + other.astype(F32)).astype(BF16)
    with jax.named_scope("replicate"):
        every = exchange(jnp.broadcast_to(summed[None], (ny * nc, piece, HEAD)), ("y", "c"))
        every = every.reshape(2, ny * nc // 2, piece, HEAD).transpose(0, 2, 1, 3).astype(F32)
        every = every.reshape(2, piece, ny * nc * HEAD // 2)
    return grad_queries, every[0], every[1]


def solution(mesh):
    axes = Mesh(mesh.devices.reshape(4, 8, 4, 2, 2), CTX + DP)
    by_row = P(DP, CTX, None)
    return jax.shard_map(
        on_device,
        mesh=axes,
        in_specs=(by_row, by_row, by_row, by_row, by_row, P(CTX), P(DP, None)),
        out_specs=(by_row, P(CTX, None), P(CTX, None)),
        check_vma=False,
    )
```

```python
import functools
import math

import jax
import jax.numpy as jnp
from jax import lax
from jax.experimental import pallas as pl
from jax.experimental.pallas import tpu as pltpu
from jax.sharding import Mesh, PartitionSpec as P

QUERY_HEADS = 20
KEY_VALUE_HEADS = 4
SHARING = QUERY_HEADS // KEY_VALUE_HEADS
HEAD = 128
ROWS = 128
HALF = ROWS // 2
WINDOW = 4
DOCUMENTS = 8
SCALE = HEAD ** (-0.5)
LINE = ("za", "zb")
CTX = ("x",) + LINE
DP = ("y", "zh", "c")
BF16 = jnp.bfloat16
VMEM_LIMIT = 60 * 1024 * 1024
F32 = jnp.float32


def shifted(block, distance):
    n = lax.axis_size(CTX)
    return lax.ppermute(block, CTX, [((i - distance) % n, i) for i in range(n)])


def beyond(block, second):
    nx, nz = lax.axis_size("x"), lax.axis_size(LINE)
    across = lax.ppermute(block, CTX, [(x * nz + nz - 3, (x + 1) % nx * nz) for x in range(nx)])
    along = lax.ppermute(second, LINE, [(z, z + 1) for z in range(nz - 1)])
    return jnp.where(lax.axis_index(LINE) == 0, across, along)


def returned(first, second, third):
    nx, nz = lax.axis_size("x"), lax.axis_size(LINE)
    along = lax.ppermute(third, LINE, [(z, z - 1) for z in range(1, nz)])
    across = lax.ppermute(third, CTX, [(x * nz, (x - 1) % nx * nz + nz - 3) for x in range(nx)])
    second = (second.astype(F32) + along.astype(F32)).astype(BF16)
    return shifted(first, -1), shifted(second, -2), across


def exchange(blocks, axes):
    return lax.all_to_all(blocks, axes, 0, 0, tiled=True)


def dot(a, b, ca, cb):
    return lax.dot_general(a, b, (((ca,), (cb,)), ((), ())), preferred_element_type=F32)


def attention_kernel(
    span_ref, seg_ref, q_ref, g_ref, k_ref, v_ref, t1_ref, t2_ref, t3_ref,
    dq_ref, own_ref, r1_ref, r2_ref, r3_ref, bias_ref,
):
    tiles = (t1_ref, t2_ref, t3_ref)

    @pl.when(pl.program_id(0) == 0)
    def _():
        lane = lax.broadcasted_iota(jnp.int32, (1, ROWS), 1)
        pos_q = jnp.where(lane < HALF, span_ref[0] * HALF + lane, span_ref[1] * HALF + lane - HALF)
        seg = seg_ref[...]
        start = jnp.zeros((1, ROWS), jnp.int32)
        for doc in range(1, DOCUMENTS):
            first = jnp.sum((seg < doc).astype(F32), axis=1, keepdims=True).astype(jnp.int32)
            start = jnp.maximum(start, jnp.where(first <= pos_q, first, 0))
        row = lax.broadcasted_iota(jnp.int32, (HALF, ROWS), 0)
        for step in range(WINDOW):
            for half in range(2):
                if step == 0:
                    span = span_ref[half]
                else:
                    at = 2 * ROWS + 8 * half
                    span = tiles[step - 1][at : at + 8, :].astype(F32)[0:1, :].astype(jnp.int32)
                pos_k = span * HALF + row
                allowed = (pos_k <= pos_q) & (pos_k >= start)
                at = step * ROWS + half * HALF
                bias_ref[at : at + HALF, :] = jnp.where(allowed, 0.0, -1e30)

    k = jnp.concatenate([k_ref[...]] + [t[0:ROWS, :] for t in tiles], axis=0)
    v = jnp.concatenate([v_ref[...]] + [t[ROWS : 2 * ROWS, :] for t in tiles], axis=0)
    heads = [slice(c * HEAD, (c + 1) * HEAD) for c in range(SHARING)]
    q = jnp.concatenate([q_ref[:, h] for h in heads], axis=0)
    g = jnp.concatenate([g_ref[:, h] for h in heads], axis=0)
    bias = bias_ref[...]
    s = dot(k, q, 1, 1) + jnp.concatenate([bias] * SHARING, axis=1)
    e = jnp.exp2((s - jnp.max(s, axis=0, keepdims=True)) * (SCALE * math.log2(math.e)))
    p = e * (1.0 / jnp.sum(e, axis=0, keepdims=True))
    dp = dot(v, g, 1, 1)
    delta = jnp.sum(p * dp, axis=0, keepdims=True)
    ds = (p * (dp - delta)).astype(BF16)
    dv = dot(p.astype(BF16), g, 1, 0)
    dk = dot(ds, q, 1, 0) * SCALE
    dq = (dot(ds, k, 0, 0) * SCALE).astype(BF16)
    for c, h in enumerate(heads):
        dq_ref[:, h] = dq[c * ROWS : (c + 1) * ROWS, :]
    own_ref[0] = dk[0:ROWS]
    own_ref[1] = dv[0:ROWS]
    for step, ref in enumerate((r1_ref, r2_ref, r3_ref), 1):
        rows = slice(step * ROWS, (step + 1) * ROWS)
        ref[0] = dk[rows].astype(BF16)
        ref[1] = dv[rows].astype(BF16)


def tile_kernel(span_ref, k_ref, v_ref, tile_ref):
    tile_ref[0:ROWS, :] = k_ref[0]
    tile_ref[ROWS : 2 * ROWS, :] = v_ref[0]
    row = lax.broadcasted_iota(jnp.int32, (16, tile_ref.shape[1]), 0)
    number = jnp.where(row < 8, span_ref[0], span_ref[1]).astype(F32)
    tile_ref[2 * ROWS :, :] = number.astype(BF16)


def packed_tile(span, keys, values):
    whole = pl.BlockSpec(memory_space=pltpu.VMEM)
    return pl.pallas_call(
        tile_kernel,
        in_specs=[pl.BlockSpec(memory_space=pltpu.SMEM), whole, whole],
        out_specs=whole,
        out_shape=jax.ShapeDtypeStruct((2 * ROWS + 16, keys.shape[2]), BF16),
        compiler_params=pltpu.CompilerParams(vmem_limit_bytes=VMEM_LIMIT),
        name="packed_tile",
    )(span, keys, values)


def copies_kernel(x_ref, out_ref, sems):
    parts = x_ref.shape[2] // out_ref.shape[2]
    copies = out_ref.shape[0] // parts
    width = out_ref.shape[2]
    moves = [
        pltpu.make_async_copy(
            x_ref.at[0, :, i * width : (i + 1) * width], out_ref.at[i * copies + j], sems.at[i, j]
        )
        for i in range(parts)
        for j in range(copies)
    ]
    for move in moves:
        move.start()
    for move in moves:
        move.wait()


def feature_blocks(inputs, parts, copies):
    rows, features = inputs.shape[1:]
    return pl.pallas_call(
        copies_kernel,
        in_specs=[pl.BlockSpec(memory_space=pltpu.VMEM)],
        out_specs=pl.BlockSpec(memory_space=pl.ANY),
        out_shape=jax.ShapeDtypeStruct((parts * copies, rows, features // parts), BF16),
        scratch_shapes=[pltpu.SemaphoreType.DMA((parts, copies))],
        compiler_params=pltpu.CompilerParams(vmem_limit_bytes=VMEM_LIMIT),
        cost_estimate=pl.CostEstimate(
            flops=0, bytes_accessed=4 * rows * features * copies, transcendentals=0
        ),
        name="feature_blocks",
    )(inputs)


def sum_kernel(own_ref, b1_ref, b2_ref, b3_ref, after_ref, out_ref):
    del after_ref
    total = own_ref[...]
    for ref in (b1_ref, b2_ref, b3_ref):
        total = total + ref[...].astype(F32)
    for i in range(2):
        for j in range(2):
            turned = total[i, j].T.astype(BF16)
            for copy in range(out_ref.shape[0]):
                out_ref[copy, 2 * i + j] = turned


def sum_terms(own, back, copies, after):
    whole = pl.BlockSpec(memory_space=pltpu.VMEM)
    return pl.pallas_call(
        sum_kernel,
        in_specs=[whole] * 4 + [pl.BlockSpec(memory_space=pl.ANY)],
        out_specs=whole,
        out_shape=jax.ShapeDtypeStruct((copies, 4, own.shape[3], own.shape[2]), BF16),
        compiler_params=pltpu.CompilerParams(vmem_limit_bytes=VMEM_LIMIT),
        cost_estimate=pl.CostEstimate(
            flops=own.size * 4, bytes_accessed=own.size * 18, transcendentals=0
        ),
        name="sum_terms",
    )(own, *back, after)


def attention(span, segments, queries, gradient, keys, values, tiles):
    wide = pl.BlockSpec((None, ROWS, SHARING * HEAD), lambda i: (0, 0, i))
    narrow = pl.BlockSpec((None, ROWS, HEAD), lambda i: (0, 0, i))
    tile = pl.BlockSpec((tiles[0].shape[0], HEAD), lambda i: (0, i))
    term = pl.BlockSpec((2, None, ROWS, HEAD), lambda i: (0, i // 2, 0, i % 2))
    terms = (2, 2, ROWS, 2 * HEAD)
    work = QUERY_HEADS * ROWS * WINDOW * ROWS
    return pl.pallas_call(
        attention_kernel,
        grid=(KEY_VALUE_HEADS,),
        in_specs=[
            pl.BlockSpec(memory_space=pltpu.SMEM),
            pl.BlockSpec(segments.shape, lambda i: (0, 0)),
            wide, wide, narrow, narrow, tile, tile, tile,
        ],
        out_specs=[wide, term, term, term, term],
        out_shape=[
            jax.ShapeDtypeStruct(queries.shape, BF16),
            jax.ShapeDtypeStruct(terms, F32),
            jax.ShapeDtypeStruct(terms, BF16),
            jax.ShapeDtypeStruct(terms, BF16),
            jax.ShapeDtypeStruct(terms, BF16),
        ],
        scratch_shapes=[pltpu.VMEM((WINDOW * ROWS, ROWS), F32)],
        compiler_params=pltpu.CompilerParams(vmem_limit_bytes=VMEM_LIMIT),
        cost_estimate=pl.CostEstimate(
            flops=10 * HEAD * work, bytes_accessed=5 * 1024 * 1024, transcendentals=work
        ),
        name="attention",
    )(span, segments, queries, gradient, keys, values, *tiles)


def on_device(queries, keys, values, output_gradient, inputs, span_ids, segments):
    nx, ny, na, nb, nzh, nc = (lax.axis_size(a) for a in ("x", "y", "za", "zb", "zh", "c"))
    rows, features = inputs.shape[1:]
    part = features // nx
    with jax.named_scope("keys_values_halo"):
        tile = packed_tile(span_ids, keys, values)
        tiles = [shifted(tile, 1), shifted(tile, 2)]
        tiles.append(beyond(tile, lax.optimization_barrier((tiles[1], tiles[0]))[0]))
    with jax.named_scope("inputs_exchange"):
        blocks = feature_blocks(inputs, nx, ny)
        features_x = exchange(blocks, ("x", "y"))
    with jax.named_scope("attention"):
        grad_queries, own, *terms = attention(
            span_ids, segments, queries, output_gradient, keys, values, tiles
        )
    with jax.named_scope("gradient_return"):
        back = returned(*terms)
        blocks = sum_terms(own, back, nx, features_x)
    with jax.named_scope("gradient_exchange"):
        columns = exchange(blocks.reshape(nx * ny, 2 * HEAD, rows), ("x", "y"))
    with jax.named_scope("projection"):
        partial = jnp.einsum("bcr,brf->cf", columns, features_x, preferred_element_type=F32)
    with jax.named_scope("core_sum"):
        halves = exchange(partial.astype(BF16).reshape(nc, HEAD, part), ("c",))
        pair = jnp.sum(halves.astype(F32), axis=0).astype(BF16)
    with jax.named_scope("z_sum"):
        piece = part // (na * nb)
        pieces = pair.T.reshape(na, nb, piece, HEAD).transpose(1, 0, 2, 3)
        pieces = exchange(pieces, ("zb",))
        summed = jnp.sum(pieces.astype(F32), axis=0).astype(BF16)
        pieces = jnp.broadcast_to(summed[None], (nzh, na, piece, HEAD))
        pieces = exchange(pieces.reshape(nzh * na, piece, HEAD), ("zh", "za"))
        summed = jnp.sum(pieces.astype(F32), axis=0).astype(BF16)
    with jax.named_scope("replicate"):
        every = exchange(jnp.broadcast_to(summed[None], (ny * nc, piece, HEAD)), ("y", "c"))
        every = every.reshape(2, ny * nc // 2, piece, HEAD).transpose(0, 2, 1, 3).astype(F32)
        every = every.reshape(2, piece, ny * nc * HEAD // 2)
    return grad_queries, every[0], every[1]


def solution(mesh):
    axes = Mesh(mesh.devices.reshape(4, 2, 4, 4, 2, 2), CTX + DP)
    by_row = P(DP, CTX, None)
    return jax.shard_map(
        on_device,
        mesh=axes,
        in_specs=(by_row, by_row, by_row, by_row, by_row, P(CTX), P(DP, None)),
        out_specs=(by_row, P(CTX, None), P(CTX, None)),
        check_vma=False,
    )
```

```python
import functools
import math

import jax
import jax.numpy as jnp
from jax import lax
from jax.experimental import pallas as pl
from jax.experimental.pallas import tpu as pltpu
from jax.sharding import Mesh, PartitionSpec as P

QUERY_HEADS = 20
KEY_VALUE_HEADS = 4
SHARING = QUERY_HEADS // KEY_VALUE_HEADS
HEAD = 128
ROWS = 128
HALF = ROWS // 2
WINDOW = 4
DOCUMENTS = 8
PER_STEP = 4
SCALE = HEAD ** (-0.5)
LINE = ("za", "zb")
CTX = ("x",) + LINE
DP = ("y", "zh", "c")
BF16 = jnp.bfloat16
VMEM_LIMIT = 60 * 1024 * 1024
F32 = jnp.float32


def shifted(block, distance):
    n = lax.axis_size(CTX)
    return lax.ppermute(block, CTX, [((i - distance) % n, i) for i in range(n)])


def beyond(block, second):
    nx, nz = lax.axis_size("x"), lax.axis_size(LINE)
    across = lax.ppermute(block, CTX, [(x * nz + nz - 3, (x + 1) % nx * nz) for x in range(nx)])
    along = lax.ppermute(second, LINE, [(z, z + 1) for z in range(nz - 1)])
    return along, across


def returned(first, second, third):
    nx, nz = lax.axis_size("x"), lax.axis_size(LINE)
    along = lax.ppermute(third, LINE, [(z, z - 1) for z in range(1, nz)])
    across = lax.ppermute(third, CTX, [(x * nz, (x - 1) % nx * nz + nz - 3) for x in range(nx)])
    second = (second.astype(F32) + along.astype(F32)).astype(BF16)
    return shifted(first, -1), shifted(second, -2), across


def neighbours(block, axis):
    n = lax.axis_size(axis)
    return tuple(lax.ppermute(block, axis, [(i, (i + by) % n) for i in range(n)]) for by in (1, -1))


def opposite(before, after, axis):
    return neighbours(before, axis)[0], neighbours(after, axis)[1]


def settled(first, second):
    anywhere = pl.BlockSpec(memory_space=pl.ANY)
    return pl.pallas_call(
        lambda *refs: None,
        in_specs=[anywhere] * 2,
        out_specs=[anywhere] * 2,
        out_shape=[jax.ShapeDtypeStruct(a.shape, a.dtype) for a in (first, second)],
        input_output_aliases={0: 0, 1: 1},
        compiler_params=pltpu.CompilerParams(vmem_limit_bytes=VMEM_LIMIT),
        cost_estimate=pl.CostEstimate(flops=30000000000, bytes_accessed=0, transcendentals=0),
        name="settled",
    )(first, second)


def exchange(blocks, axes):
    return lax.all_to_all(blocks, axes, 0, 0, tiled=True)


def dot(a, b, ca, cb):
    return lax.dot_general(a, b, (((ca,), (cb,)), ((), ())), preferred_element_type=F32)


def attention_kernel(
    span_ref, seg_ref, q_ref, g_ref, k_ref, v_ref, t1_ref, t2_ref, along_ref, across_ref,
    dq_ref, own_ref, r1_ref, r2_ref, r3_ref, bias_ref,
):
    placed = {1: (t1_ref,), 2: (t2_ref,), 3: (along_ref, across_ref)}

    @pl.when(pl.program_id(0) == 0)
    def _():
        lane = lax.broadcasted_iota(jnp.int32, (1, ROWS), 1)
        pos_q = jnp.where(lane < HALF, span_ref[0] * HALF + lane, span_ref[1] * HALF + lane - HALF)
        seg = seg_ref[...]
        start = jnp.zeros((1, ROWS), jnp.int32)
        for doc in range(1, DOCUMENTS):
            first = jnp.sum((seg < doc).astype(F32), axis=1, keepdims=True).astype(jnp.int32)
            start = jnp.maximum(start, jnp.where(first <= pos_q, first, 0))
        row = lax.broadcasted_iota(jnp.int32, (HALF, ROWS), 0)
        for step in range(WINDOW):
            for half in range(2):
                if step == 0:
                    span = span_ref[half]
                else:
                    at = 2 * ROWS + 8 * half
                    span = sum(t[at : at + 8, 0:ROWS].astype(F32) for t in placed[step])
                    span = span[0:1, :].astype(jnp.int32)
                pos_k = span * HALF + row
                allowed = (pos_k <= pos_q) & (pos_k >= start)
                at = step * ROWS + half * HALF
                bias_ref[at : at + HALF, :] = jnp.where(allowed, 0.0, -1e30)

    for head in range(q_ref.shape[1] // (SHARING * HEAD)):
        own = slice(head * HEAD, (head + 1) * HEAD)
        k, v = (
            jnp.concatenate(
                [first[:, own], t1_ref[rows, own], t2_ref[rows, own]]
                + [along_ref[rows, own] + across_ref[rows, own]],
                axis=0,
            )
            for first, rows in ((k_ref, slice(0, ROWS)), (v_ref, slice(ROWS, 2 * ROWS)))
        )
        heads = [
            slice(c * HEAD, (c + 1) * HEAD) for c in range(head * SHARING, (head + 1) * SHARING)
        ]
        q = jnp.concatenate([q_ref[:, h] for h in heads], axis=0)
        g = jnp.concatenate([g_ref[:, h] for h in heads], axis=0)
        bias = bias_ref[...]
        s = dot(k, q, 1, 1) + jnp.concatenate([bias] * SHARING, axis=1)
        e = jnp.exp2((s - jnp.max(s, axis=0, keepdims=True)) * (SCALE * math.log2(math.e)))
        p = e * (1.0 / jnp.sum(e, axis=0, keepdims=True))
        dp = dot(v, g, 1, 1)
        delta = jnp.sum(p * dp, axis=0, keepdims=True)
        ds = (p * (dp - delta)).astype(BF16)
        dv = dot(p.astype(BF16), g, 1, 0)
        dk = dot(ds, q, 1, 0) * SCALE
        dq = (dot(k, ds, 0, 0) * SCALE).T.astype(BF16)
        for c, h in enumerate(heads):
            dq_ref[:, h] = dq[c * ROWS : (c + 1) * ROWS, :]
        pair, at = head // 2, slice(head % 2 * HEAD, (head % 2 + 1) * HEAD)
        own_ref[0, pair, :, at] = dk[0:ROWS]
        own_ref[1, pair, :, at] = dv[0:ROWS]
        for step, ref in enumerate((r1_ref, r2_ref, r3_ref), 1):
            rows = slice(step * ROWS, (step + 1) * ROWS)
            ref[0, pair, :, at] = dk[rows].astype(BF16)
            ref[1, pair, :, at] = dv[rows].astype(BF16)


def tile_kernel(span_ref, k_ref, v_ref, tile_ref):
    tile_ref[0:ROWS, :] = k_ref[0]
    tile_ref[ROWS : 2 * ROWS, :] = v_ref[0]
    row = lax.broadcasted_iota(jnp.int32, (16, tile_ref.shape[1]), 0)
    number = jnp.where(row < 8, span_ref[0], span_ref[1]).astype(F32)
    tile_ref[2 * ROWS :, :] = number.astype(BF16)


def packed_tile(span, keys, values):
    whole = pl.BlockSpec(memory_space=pltpu.VMEM)
    return pl.pallas_call(
        tile_kernel,
        in_specs=[pl.BlockSpec(memory_space=pltpu.SMEM), whole, whole],
        out_specs=whole,
        out_shape=jax.ShapeDtypeStruct((2 * ROWS + 16, keys.shape[2]), BF16),
        compiler_params=pltpu.CompilerParams(vmem_limit_bytes=VMEM_LIMIT),
        name="packed_tile",
    )(span, keys, values)


def copies_kernel(x_ref, out_ref, sems):
    parts = x_ref.shape[2] // out_ref.shape[2]
    copies = out_ref.shape[0] // parts
    width = out_ref.shape[2]
    moves = [
        pltpu.make_async_copy(
            x_ref.at[0, :, i * width : (i + 1) * width], out_ref.at[i * copies + j], sems.at[i, j]
        )
        for i in range(parts)
        for j in range(copies)
    ]
    for move in moves:
        move.start()
    for move in moves:
        move.wait()


def feature_blocks(inputs, parts, copies):
    rows, features = inputs.shape[1:]
    return pl.pallas_call(
        copies_kernel,
        in_specs=[pl.BlockSpec(memory_space=pltpu.VMEM)],
        out_specs=pl.BlockSpec(memory_space=pl.ANY),
        out_shape=jax.ShapeDtypeStruct((parts * copies, rows, features // parts), BF16),
        scratch_shapes=[pltpu.SemaphoreType.DMA((parts, copies))],
        compiler_params=pltpu.CompilerParams(vmem_limit_bytes=VMEM_LIMIT),
        cost_estimate=pl.CostEstimate(
            flops=0, bytes_accessed=4 * rows * features * copies, transcendentals=0
        ),
        name="feature_blocks",
    )(inputs)


def sum_kernel(own_ref, b1_ref, b2_ref, b3_ref, *refs):
    out_ref = refs[-1]
    total = own_ref[...]
    for ref in (b1_ref, b2_ref, b3_ref):
        total = total + ref[...].astype(F32)
    for i in range(2):
        for j in range(2):
            turned = total[i, j].T.astype(BF16)
            for copy in range(out_ref.shape[1]):
                out_ref[2 * i + j, copy] = turned


def sum_terms(own, back, copies, after):
    whole = pl.BlockSpec(memory_space=pltpu.VMEM)
    return pl.pallas_call(
        sum_kernel,
        in_specs=[whole] * 4 + [pl.BlockSpec(memory_space=pl.ANY)] * len(after),
        out_specs=whole,
        out_shape=jax.ShapeDtypeStruct((4, copies, own.shape[3], own.shape[2]), BF16),
        compiler_params=pltpu.CompilerParams(vmem_limit_bytes=VMEM_LIMIT),
        cost_estimate=pl.CostEstimate(
            flops=20000000000, bytes_accessed=own.size * 18, transcendentals=0
        ),
        name="sum_terms",
    )(own, *back, *after)


def attention(span, segments, queries, gradient, keys, values, tiles):
    wide = pl.BlockSpec((None, ROWS, PER_STEP * SHARING * HEAD), lambda i: (0, 0, i))
    narrow = pl.BlockSpec((None, ROWS, PER_STEP * HEAD), lambda i: (0, 0, i))
    tile = pl.BlockSpec((tiles[0].shape[0], PER_STEP * HEAD), lambda i: (0, i))
    term = pl.BlockSpec((2, PER_STEP // 2, ROWS, 2 * HEAD), lambda i: (0, i, 0, 0))
    terms = (2, 2, ROWS, 2 * HEAD)
    work = QUERY_HEADS * ROWS * WINDOW * ROWS
    return pl.pallas_call(
        attention_kernel,
        grid=(KEY_VALUE_HEADS // PER_STEP,),
        in_specs=[
            pl.BlockSpec(memory_space=pltpu.SMEM),
            pl.BlockSpec(segments.shape, lambda i: (0, 0)),
            wide, wide, narrow, narrow, tile, tile, tile, tile,
        ],
        out_specs=[wide, term, term, term, term],
        out_shape=[
            jax.ShapeDtypeStruct(queries.shape, BF16),
            jax.ShapeDtypeStruct(terms, F32),
            jax.ShapeDtypeStruct(terms, BF16),
            jax.ShapeDtypeStruct(terms, BF16),
            jax.ShapeDtypeStruct(terms, BF16),
        ],
        scratch_shapes=[pltpu.VMEM((WINDOW * ROWS, ROWS), F32)],
        compiler_params=pltpu.CompilerParams(vmem_limit_bytes=24 * 1024 * 1024),
        cost_estimate=pl.CostEstimate(
            flops=60 * HEAD * work, bytes_accessed=5 * 1024 * 1024, transcendentals=work
        ),
        name="attention",
    )(span, segments, queries, gradient, keys, values, *tiles)


def on_device(queries, keys, values, output_gradient, inputs, span_ids, segments):
    nx, ny, na, nb, nzh, nc = (lax.axis_size(a) for a in ("x", "y", "za", "zb", "zh", "c"))
    rows, features = inputs.shape[1:]
    part = features // nx
    with jax.named_scope("keys_values_halo"):
        tile = packed_tile(span_ids, keys, values)
        tiles = [shifted(tile, 1), shifted(tile, 2)]
        tiles.extend(beyond(tile, lax.optimization_barrier((tiles[1], tiles[0]))[0]))
    with jax.named_scope("inputs_exchange"):
        held = exchange(feature_blocks(inputs, nx, 1), ("x",))
        held, *_ = lax.optimization_barrier((held, *tiles[:2]))
        before, after = neighbours(held, "y")
    with jax.named_scope("attention"):
        grad_queries, own, *terms = attention(
            span_ids, segments, queries, output_gradient, keys, values, tiles
        )
    with jax.named_scope("gradient_return"):
        back = returned(*terms)
        halves = before[: nx // 2], after[nx // 2 :]
        blocks = sum_terms(own, back, nx, halves)
    with jax.named_scope("gradient_exchange"):
        columns = exchange(blocks.reshape(ny * nx, 2 * HEAD, rows), ("y", "x"))
    with jax.named_scope("projection"):
        me = lax.axis_index("y")
        columns = columns.reshape(ny, nx, 2 * HEAD, rows)
        across_y = settled(*opposite(*halves, "y"))
        columns, *across_y = lax.optimization_barrier((columns, *across_y))
        features_x = held, after, across_y, before
        partial = jnp.zeros((2 * HEAD, part), F32)
        for step in (0, 1, 3, 2):
            blocks = features_x[step]
            match = lax.dynamic_index_in_dim(columns, (me + step) % ny, 0, keepdims=False)
            blocks = jnp.concatenate(blocks, axis=0) if step == 2 else blocks
            partial += jnp.einsum("bcr,brf->cf", match, blocks, preferred_element_type=F32)
    with jax.named_scope("core_sum"):
        halves = exchange(partial.astype(BF16).reshape(nc, HEAD, part), ("c",))
        pair = jnp.sum(halves.astype(F32), axis=0).astype(BF16)
    with jax.named_scope("z_sum"):
        piece = part // (na * nb)
        pieces = pair.T.reshape(na, nb, piece, HEAD).transpose(1, 0, 2, 3)
        pieces = exchange(pieces, ("zb",))
        summed = jnp.sum(pieces.astype(F32), axis=0).astype(BF16)
        pieces = jnp.broadcast_to(summed[None], (nzh, na, piece, HEAD))
        pieces = exchange(pieces.reshape(nzh * na, piece, HEAD), ("zh", "za"))
        summed = jnp.sum(pieces.astype(F32), axis=0).astype(BF16)
    with jax.named_scope("replicate"):
        every = exchange(jnp.broadcast_to(summed[None], (ny * nc, piece, HEAD)), ("y", "c"))
        every = every.reshape(2, ny * nc // 2, piece, HEAD).transpose(0, 2, 1, 3).astype(F32)
        every = every.reshape(2, piece, ny * nc * HEAD // 2)
    return grad_queries, every[0], every[1]


def solution(mesh):
    axes = Mesh(mesh.devices.reshape(4, 2, 4, 4, 2, 2), CTX + DP)
    by_row = P(DP, CTX, None)
    return jax.shard_map(
        on_device,
        mesh=axes,
        in_specs=(by_row, by_row, by_row, by_row, by_row, P(CTX), P(DP, None)),
        out_specs=(by_row, P(CTX, None), P(CTX, None)),
        check_vma=False,
    )
```
